32 devices in a mesh: gx: 2 (over y), gy: 4 (over z), gz: 4 (over x, core).
Axes of the slice: x: 2, y: 2, z: 4, core: 2. Of those that a mesh axis runs over, the one named last changes fastest.
Arguments:
- views: float32 [6, 16, 64, 512], P(None, 'gx', ('gy', 'gz')), may hold values from 0.2 to 5
- estimate: float32 [16, 64, 512], P('gx', 'gy', 'gz'), may hold values from 0.5 to 2
- psf: float32 [6, 3, 17], replicated, may hold values from 0.2 to 1
- extents: int32 [6, 3, 2], replicated, may hold values from 0 to 512, as said below
Outputs:
- deconvolved: float32 [16, 64, 512], P('gx', 'gy', 'gz')
The draws below stay inside these ranges and needn't reach their ends.
Inputs may be any that keep to these rules, and one draw needn't show every extreme that they name: extents[v, a, 0] < extents[v, a, 1] <= the number of cells along axis a (16, 64, 512 for a = 0, 1, 2).
All inputs are finite; a program needn't handle non-finite values.
Results may differ from the reference program's by a relative error of at most 0.0003.
Values sent between devices are 32-bit elements; how exact they have to be, the bound alone decides.
A program may use at most 64 MiB of HBM per device.

```python
import math
import jax
import jax.numpy as jnp
from jax import lax

V = 6
H = 8
K = 17
ITERS = 2
NX = 16
NY = 64
NZ = 512


def draw_extents(key, part):
    first_key, second_key = jax.random.split(jax.random.fold_in(key, 17))
    cells = jnp.array([NX, NY, NZ], jnp.int32)[None, :]
    half = cells // 2
    lower_bits = jax.random.randint(first_key, (V, 3), 0, 1 << 20)
    upper_bits = jax.random.randint(second_key, (V, 3), 0, 1 << 20)
    low = lower_bits % half
    high_even = half + 1 + upper_bits % (cells - half)
    odd_view = (jnp.arange(V, dtype=jnp.int32) % 2 == 1)[:, None]
    lower = jnp.where(odd_view, low, jnp.zeros_like(low))
    upper = jnp.where(odd_view, jnp.broadcast_to(cells, (V, 3)), high_even)
    return jnp.stack([lower, upper], axis=-1).astype(jnp.int32)


def block_levels(own_key, dims, cuts, smallest, high):
    def one(axis_at, parts):
        heights = jax.random.uniform(jax.random.fold_in(jax.random.fold_in(own_key, 6), axis_at), (parts,), jnp.float32, smallest / len(cuts), high / len(cuts))
        return jnp.repeat(jnp.exp(heights), dims[axis_at] // parts).reshape((-1,) + (1,) * (len(dims) - axis_at - 1))

    gain = one(*cuts[0])
    for cut in cuts[1:]:
        gain = gain * one(*cut)
    return gain


def setup_inputs(seed: int = 0) -> dict:
    seeds = jax.random.split(jax.random.key(seed), 5)
    views = jnp.clip(jnp.exp(math.log(5.0) - 3.218876 * jax.random.uniform(seeds[0], (V, NX, NY, NZ), jnp.float32) ** block_levels(seeds[0], (V, NX, NY, NZ), ((1, 2), (2, 16)), -0.2, 0.2)), 0.2, 5.0)
    estimate = jnp.clip(jnp.exp(math.log(2.0) - 1.3862944 * jax.random.uniform(seeds[1], (NX, NY, NZ), jnp.float32) ** block_levels(seeds[1], (NX, NY, NZ), ((0, 2), (1, 4), (2, 4)), -0.2, 0.2)), 0.5, 2.0)
    psf = jnp.clip(jnp.exp(jax.random.uniform(seeds[2], (V, 3, K), jnp.float32, math.log(0.2), math.log(1.0))), 0.2, 1.0)
    extents = draw_extents(jax.random.fold_in(seeds[4], 71), 0)
    return dict(views=views, estimate=estimate, psf=psf, extents=extents)


def blur_axis(volume, kernel, axis):
    length = volume.shape[axis]
    widths = [(0, 0), (0, 0), (0, 0)]
    widths[axis] = (H, H)
    padded = jnp.pad(volume, widths)
    total = kernel[0] * lax.slice_in_dim(padded, 0, length, axis=axis)
    for tap in range(1, K):
        total = total + kernel[tap] * lax.slice_in_dim(padded, tap, tap + length, axis=axis)
    return total


def blur_three(volume, kernels):
    for axis in range(3):
        volume = blur_axis(volume, kernels[axis], axis)
    return volume


def weight_of(bounds):
    first = jnp.arange(NX, dtype=jnp.int32)[:, None, None]
    second = jnp.arange(NY, dtype=jnp.int32)[None, :, None]
    third = jnp.arange(NZ, dtype=jnp.int32)[None, None, :]
    inside = (first >= bounds[0, 0]) & (first < bounds[0, 1])
    inside = inside & (second >= bounds[1, 0]) & (second < bounds[1, 1])
    inside = inside & (third >= bounds[2, 0]) & (third < bounds[2, 1])
    return jnp.where(inside, jnp.float32(1.0), jnp.float32(0.25))


def reference(views, estimate, psf, extents):
    taps = psf / jnp.sum(psf, axis=-1, keepdims=True)
    flipped = taps[:, :, ::-1]
    deconvolved = estimate

    for step in range(ITERS):
        def one_view(carry, inputs):
            image, kernels, back_kernels, bounds = inputs
            blurred = blur_three(deconvolved, kernels)
            ratio = image / blurred
            back = blur_three(ratio, back_kernels)
            weight = weight_of(bounds)
            return (carry[0] + weight * back, carry[1] + weight), None

        start = (jnp.zeros((NX, NY, NZ), jnp.float32), jnp.zeros((NX, NY, NZ), jnp.float32))
        (summed, weight_sum), unused = lax.scan(one_view, start, (views, taps, flipped, extents))
        deconvolved = deconvolved * (summed / weight_sum)
    return deconvolved
```

```python
import functools

import jax
import jax.numpy as jnp
from jax import lax
from jax.experimental import pallas as pl
from jax.experimental.pallas import tpu as pltpu
from jax.sharding import PartitionSpec as P

H = 8
K = 17
ITERS = 2
MESH = pl.DeviceIdType.MESH
F32 = jnp.float32
BF16 = jnp.bfloat16
NOWHERE = -100000
INV_Y = (0, 2, 1)
ROWS = ((0, 128), (128, 64), (192, 64))


def iota(shape, dim):
    return lax.broadcasted_iota(jnp.int32, shape, dim)


def split(value):
    high = value.astype(BF16)
    low = (value - high.astype(F32)).astype(BF16)
    return high, low


def wide(value):
    high, low = split(value)
    return jnp.concatenate([high, low, high], axis=1)


def tall(value):
    high, low = split(value)
    return jnp.concatenate([high, high, low], axis=0)


def z_place(index):
    return jnp.where(
        index < 128 + H,
        index,
        jnp.where(index < 128 + 2 * H, index - 128 - 2 * H, NOWHERE),
    )


def y_place(index):
    return jnp.where(index < 24, index, index - 32)


def pick(offset, tap):
    total = jnp.zeros(offset.shape, F32)
    for t in range(K):
        total = jnp.where(offset == t, tap(t), total)
    return total


def kernel(
    sizes, psf_ref, extents_ref, views_ref, est_ref, out_ref,
    images, image, forth, back, z_forth, z_back, weights, u_ref, z_ref, z_own, s_ref, sz_ref,
    rc_ref, rz_ref, zc_ref, rz2_ref, view_send, view_recv, send, recv, z_send, z_recv,
):
    n_gx, n_gy, n_gz = sizes
    V = image.shape[0]
    gx, gy, gz = lax.axis_index("gx"), lax.axis_index("gy"), lax.axis_index("gz")
    if n_gx == 2:
        x_targets = (gx, 1 - gx)
        x_exists = (None, None)
        x_offset = (0, H - 2 * H * gx)
        inv_x = (0, 1)
    else:
        x_targets = (gx, gx + 1, gx - 1)
        x_exists = (None, gx < n_gx - 1, gx > 0)
        x_offset = (0, H, -H)
        inv_x = (0, 2, 1)
    slots = len(x_targets)
    y_targets = (gy, gy + 1, gy - 1)
    y_exists = (None, gy < n_gy - 1, gy > 0)
    z_targets = (gz + 1, gz - 1)
    z_exists = (gz < n_gz - 1, gz > 0)
    near = []
    for s in range(slots):
        for y in range(3):
            if s == 0 and y == 0:
                continue
            exists = x_exists[s]
            if y_exists[y] is not None:
                exists = y_exists[y] if exists is None else exists & y_exists[y]
            near.append((s, y, exists, {"gx": x_targets[s], "gy": y_targets[y], "gz": gz}))
    started = []

    def under(exists, do):
        if exists is None:
            do()
        else:
            pl.when(exists)(do)

    def start(exists, make):
        under(exists, lambda: make().start())
        started.append((exists, make))

    def remote(src, dst, s_sem, r_sem, device):
        return lambda: pltpu.make_async_remote_copy(
            src_ref=src, dst_ref=dst, send_sem=s_sem, recv_sem=r_sem,
            device_id=device, device_id_type=MESH,
        )

    barrier = pltpu.get_barrier_semaphore()
    expected = jnp.int32(n_gz - 1)
    for k in range(1, n_gz):
        pl.semaphore_signal(
            barrier, inc=1, device_id={"gx": gx, "gy": gy, "gz": lax.rem(gz + k, n_gz)},
            device_id_type=MESH,
        )
    for s, y, exists, device in near:
        under(exists, functools.partial(
            pl.semaphore_signal, barrier, inc=1, device_id=device, device_id_type=MESH))
        expected = expected + (1 if exists is None else exists.astype(jnp.int32))

    own_views = pltpu.make_async_copy(
        views_ref.at[:, :, :, pl.ds(pl.multiple_of(gz * 128, 128), 128)],
        images.at[gz], view_recv.at[0],
    )
    own_views.start()

    for y in range(16):
        u_ref[0, 0, 8 * y:8 * y + 8, :] = est_ref[:, y, :]
    estimate = u_ref[0, 0, 0:128, :]

    def zero_z(side):
        for it in range(ITERS):
            first = 8 * side
            z_ref[it, 0, 0, first:first + 8, :] = jnp.zeros((8, 128), F32)
            rz2_ref[it, 8 - first:16 - first, :] = jnp.zeros((8, 128), F32)

    for side in range(2):
        pl.when(jnp.logical_not(z_exists[side]))(functools.partial(zero_z, side))

    def zero_near(s, y):
        first, count = ROWS[y]
        for it in range(ITERS):
            u_ref[it, s, first:first + count, :] = jnp.zeros((count, 128), F32)
            z_ref[it, s, y] = jnp.zeros((16, 128), F32)
            rc_ref[it, s, y, 0:count, :] = jnp.zeros((count, 128), F32)
            rz_ref[it, s, y] = jnp.zeros((16, 128), F32)

    for s, y, exists, device in near:
        if exists is not None:
            pl.when(jnp.logical_not(exists))(functools.partial(zero_near, s, y))

    def send_estimate(it, value):
        turned = value.T
        z_own[it, 0:8, :] = turned[0:8]
        z_own[it, 8:16, :] = turned[120:128]
        if it == 0:
            pl.semaphore_wait(barrier, expected)
        for side in (0, 1):
            rows = pl.ds(8 - 8 * side, 8)
            start(z_exists[side], remote(
                z_own.at[it, rows], z_ref.at[it, 0, 0, rows],
                z_send.at[it, 0, side], z_recv.at[it, 0, 1 - side],
                {"gx": gx, "gy": gy, "gz": z_targets[side]}))
        for s, y, exists, device in near:
            source = (0, 64, 0)[y]
            first, count = ROWS[INV_Y[y]]
            start(exists, remote(
                u_ref.at[it, 0, pl.ds(source, count)],
                u_ref.at[it, inv_x[s], pl.ds(first, count)],
                send.at[it, 0, 0, s, y], recv.at[it, 0, 0, inv_x[s], INV_Y[y]], device))

    def pass_z(it):
        for side in (0, 1):
            rows = pl.ds(8 * side, 8)
            under(z_exists[side], lambda rows=rows, side=side: remote(
                z_own.at[it, rows], z_ref.at[it, 0, 0, rows],
                z_send.at[it, 0, side], z_recv.at[it, 0, side],
                {"gx": gx, "gy": gy, "gz": z_targets[side]})().wait_recv())
        for s, y, exists, device in near:
            start(exists, remote(
                z_ref.at[it, 0, 0], z_ref.at[it, inv_x[s], INV_Y[y]],
                send.at[it, 0, 1, s, y], recv.at[it, 0, 1, inv_x[s], INV_Y[y]], device))

    send_estimate(0, estimate)
    for k in range(1, n_gz):
        target = lax.rem(gz + k, n_gz)
        start(None, remote(
            views_ref.at[:, :, :, pl.ds(pl.multiple_of(target * 128, 128), 128)],
            images.at[gz], view_send.at[k], view_recv.at[k],
            {"gx": gx, "gy": gy, "gz": target}))

    def build(v, unused):
        def taps(axis):
            return lambda t: psf_ref[v, axis * K + t]

        scale = jnp.float32(1.0)
        for axis in range(3):
            total = psf_ref[v, axis * K]
            for t in range(1, K):
                total = total + psf_ref[v, axis * K + t]
            scale = scale * total
        inverse = 1.0 / jnp.full((8, 128), scale, F32)
        z_band = pick(z_place(iota((144, 128), 0)) - iota((144, 128), 1) + H, taps(2))
        z_band = z_band * inverse[0:1]
        z_band = jnp.concatenate([z_band, jnp.zeros((112, 128), F32)], axis=0)
        z_forth[v] = tall(z_band)
        z_band_t = jnp.concatenate([z_band[0:128].T, z_band[128:256].T], axis=1)
        z_back[v] = tall(z_band_t)
        lane = iota((16, 256), 1)
        y_rows = pick(y_place(lane // 8) - iota((16, 256), 0) + H, taps(1))
        y_rows_t = pick(y_place(iota((32, 128), 0)) - iota((32, 128), 1) // 8 + H, taps(1))
        row = iota((8, 128), 0)
        column = iota((8, 128), 1) % 8
        for s in range(slots):
            x_tile = pick(x_offset[s] + column - row + H, taps(0))
            x_tile_t = pick(x_offset[s] + row - column + H, taps(0))
            for group in range(2):
                block = y_rows[:, None, 128 * group:128 * group + 128] * x_tile[None]
                high, low = split(block.reshape(128, 128))
                first = s * 256 + group * 128
                width = slots * 256
                forth[v, :, first:first + 128] = high
                forth[v, :, width + first:width + first + 128] = low
                forth[v, :, 2 * width + first:2 * width + first + 128] = high
                block = y_rows_t[16 * group:16 * group + 16, None, :] * x_tile_t[None]
                high, low = split(block.reshape(128, 128))
                back[v, first:first + 128, 0:128] = high
                back[v, first:first + 128, 128:256] = low
                back[v, first:first + 128, 256:384] = high
        z_abs = gz * 128 + z_place(iota((8, 256), 1))
        in_z = (z_abs >= extents_ref[v, 4]) & (z_abs < extents_ref[v, 5])
        z_part = jnp.where(in_z, F32(0.75), F32(0.0))[0:1]
        for s in range(slots):
            rows = iota((256, 128), 0)
            y_abs = gy * 16 + y_place(rows // 8)
            x_abs = gx * 8 + x_offset[s] + rows % 8
            inside = (y_abs >= extents_ref[v, 2]) & (y_abs < extents_ref[v, 3])
            inside = inside & (x_abs >= extents_ref[v, 0]) & (x_abs < extents_ref[v, 1])
            flag = jnp.where(inside, F32(1.0), F32(0.0))
            weights[v, s * 256:s * 256 + 256, 0:128] = flag * z_part[:, 0:128] + 0.25
            weights[v, s * 256:s * 256 + 256, 128:256] = flag * z_part[:, 128:256] + 0.25
        return unused

    pass_z(0)
    lax.fori_loop(0, V, build, 0)
    weight_sum = weights[0, 0:128, 0:128]
    for v in range(1, V):
        weight_sum = weight_sum + weights[v, 0:128, 0:128]

    half = iota((16, 128), 1) < 64
    for it in range(ITERS):
        for s, y, exists, device in near:
            first, count = ROWS[y]
            under(exists, lambda s=s, y=y, first=first, count=count, device=device: remote(
                u_ref.at[it, s, pl.ds(first, count)], u_ref.at[it, s, pl.ds(first, count)],
                send.at[it, 0, 0, s, y], recv.at[it, 0, 0, s, y], device)().wait_recv())
        for s, y, exists, device in near:
            under(exists, lambda s=s, y=y, device=device: remote(
                z_ref.at[it, s, y], z_ref.at[it, s, y],
                send.at[it, 0, 1, s, y], recv.at[it, 0, 1, s, y], device)().wait_recv())
        pieces = []
        fill = jnp.zeros((112, 128), F32)
        for s in range(slots):
            halo = jnp.where(half, z_ref[it, s, 1], z_ref[it, s, 2])
            for group, strip in enumerate((z_ref[it, s, 0], halo)):
                turned = jnp.concatenate([strip, fill], axis=0).T
                middle = u_ref[it, s, 128 * group:128 * group + 128, :]
                pieces.append(jnp.concatenate([middle, turned], axis=1))
        padded = tall(jnp.concatenate(pieces, axis=0))
        blurred = []
        for v in range(V):
            across = jnp.dot(forth[v], padded, preferred_element_type=F32)
            blurred.append(jnp.dot(wide(across), z_forth[v], preferred_element_type=F32))
        if it == 0:
            own_views.wait()
            for k in range(1, n_gz):
                remote(
                    images.at[0], images.at[lax.rem(gz + n_gz - k, n_gz)],
                    view_send.at[k], view_recv.at[k],
                    {"gx": gx, "gy": gy, "gz": lax.rem(gz + n_gz - k, n_gz)})().wait_recv()
            per = 16 // n_gz
            for v in range(V):
                for g in range(n_gz):
                    for yy in range(per):
                        first = 8 * (per * g + yy)
                        image[v, first:first + 8, :] = images[g, v, :, yy, :]
        spread = []
        for v in range(V):
            ratio = image[v] / blurred[v]
            lines = jnp.dot(wide(ratio), z_back[v], preferred_element_type=F32)
            spread.append(tall(lines))

        def summed(first):
            total = None
            for v in range(V):
                part = jnp.dot(
                    back[v, first:first + 128, :], spread[v], preferred_element_type=F32)
                part = part * weights[v, first:first + 128, :]
                total = part if total is None else total + part
            return total

        for s in range(slots - 1, -1, -1):
            for group in (1, 0):
                total = summed(s * 256 + group * 128)
                if s == 0 and group == 0:
                    own_total = total[:, 0:128]
                    own_z = total[:, 128:256].T[0:16]
                    continue
                s_ref[it, s, 128 * group:128 * group + 128, :] = total[:, 0:128]
                sz_ref[it, s, group] = total[:, 128:256].T[0:16]
                for t, y, exists, device in near:
                    if t != s or (y > 0) != (group == 1):
                        continue
                    first, count = ROWS[y]
                    start(exists, remote(
                        sz_ref.at[it, s, group], rz_ref.at[it, inv_x[s], INV_Y[y]],
                        send.at[it, 1, 1, s, y], recv.at[it, 1, 1, inv_x[s], INV_Y[y]], device))
                    start(exists, remote(
                        s_ref.at[it, s, pl.ds(first, count)],
                        rc_ref.at[it, inv_x[s], INV_Y[y], pl.ds(0, count)],
                        send.at[it, 1, 0, s, y], recv.at[it, 1, 0, inv_x[s], INV_Y[y]], device))
        for s, y, exists, device in near:
            under(exists, lambda s=s, y=y, device=device: remote(
                rz_ref.at[it, s, y], rz_ref.at[it, s, y],
                send.at[it, 1, 1, s, y], recv.at[it, 1, 1, s, y], device)().wait_recv())
        for s in range(slots):
            if s > 0:
                own_z = own_z + rz_ref[it, s, 0]
            own_z = own_z + jnp.where(half, rz_ref[it, s, 2], rz_ref[it, s, 1])
        zc_ref[it] = own_z
        for side in (0, 1):
            rows = pl.ds(8 * side, 8)
            start(z_exists[side], remote(
                zc_ref.at[it, rows], rz2_ref.at[it, rows],
                z_send.at[it, 1, side], z_recv.at[it, 1, side],
                {"gx": gx, "gy": gy, "gz": z_targets[side]}))
        for s, y, exists, device in near:
            count = ROWS[y][1]
            under(exists, lambda s=s, y=y, count=count, device=device: remote(
                rc_ref.at[it, s, y, pl.ds(0, count)], rc_ref.at[it, s, y, pl.ds(0, count)],
                send.at[it, 1, 0, s, y], recv.at[it, 1, 0, s, y], device)().wait_recv())
        for s in range(slots):
            if s > 0:
                own_total = own_total + rc_ref[it, s, 0]
            own_total = own_total + jnp.concatenate(
                [rc_ref[it, s, 2, 0:64, :], rc_ref[it, s, 1, 0:64, :]], axis=0)
        for side in (0, 1):
            rows = pl.ds(8 * side, 8)
            under(z_exists[1 - side], lambda rows=rows, side=side: remote(
                zc_ref.at[it, rows], rz2_ref.at[it, rows],
                z_send.at[it, 1, side], z_recv.at[it, 1, side],
                {"gx": gx, "gy": gy, "gz": z_targets[1 - side]})().wait_recv())
        edge = jnp.concatenate(
            [rz2_ref[it, 0:8, :], jnp.zeros((112, 128), F32), rz2_ref[it, 8:16, :]], axis=0)
        own_total = own_total + edge.T
        estimate = estimate * (own_total / weight_sum)
        if it < ITERS - 1:
            u_ref[it + 1, 0, 0:128, :] = estimate
            send_estimate(it + 1, estimate)
            pass_z(it + 1)
    for y in range(16):
        out_ref[:, y, :] = estimate[8 * y:8 * y + 8, :]
    for exists, make in started:
        under(exists, lambda make=make: make().wait_send())


def shards(sizes, views, estimate, psf, extents):
    n_gx, n_gy, n_gz = sizes
    V = views.shape[0]
    slots = 2 if n_gx == 2 else 3
    rows = slots * 256
    smem = pl.BlockSpec(memory_space=pltpu.SMEM)
    vmem = pl.BlockSpec(memory_space=pltpu.VMEM)
    return pl.pallas_call(
        functools.partial(kernel, sizes),
        out_shape=jax.ShapeDtypeStruct(estimate.shape, F32),
        in_specs=[smem, smem, pl.BlockSpec(memory_space=pl.ANY), vmem],
        out_specs=vmem,
        scratch_shapes=[
            pltpu.VMEM((n_gz,) + views.shape[:3] + (128,), F32),
            pltpu.VMEM((V, 128, 128), F32),
            pltpu.VMEM((V, 128, 3 * rows), BF16),
            pltpu.VMEM((V, rows, 384), BF16),
            pltpu.VMEM((V, 768, 128), BF16),
            pltpu.VMEM((V, 384, 256), BF16),
            pltpu.VMEM((V, rows, 256), F32),
            pltpu.VMEM((ITERS, slots, 256, 128), F32),
            pltpu.VMEM((ITERS, slots, 3, 16, 128), F32),
            pltpu.VMEM((ITERS, 16, 128), F32),
            pltpu.VMEM((ITERS, slots, 256, 128), F32),
            pltpu.VMEM((ITERS, slots, 2, 16, 128), F32),
            pltpu.VMEM((ITERS, slots, 3, 128, 128), F32),
            pltpu.VMEM((ITERS, slots, 3, 16, 128), F32),
            pltpu.VMEM((ITERS, 16, 128), F32),
            pltpu.VMEM((ITERS, 16, 128), F32),
            pltpu.SemaphoreType.DMA((n_gz,)),
            pltpu.SemaphoreType.DMA((n_gz,)),
            pltpu.SemaphoreType.DMA((ITERS, 2, 2, slots, 3)),
            pltpu.SemaphoreType.DMA((ITERS, 2, 2, slots, 3)),
            pltpu.SemaphoreType.DMA((ITERS, 2, 2)),
            pltpu.SemaphoreType.DMA((ITERS, 2, 2)),
        ],
        compiler_params=pltpu.CompilerParams(
            collective_id=0, has_side_effects=True, vmem_limit_bytes=40 * 1024 * 1024
        ),
    )(psf.reshape(V, 3 * K), extents.reshape(V, 6), views, estimate)


def solution(mesh):
    sizes = (mesh.shape["gx"], mesh.shape["gy"], mesh.shape["gz"])
    placed = (P(None, "gx", ("gy", "gz"), None), P("gx", "gy", "gz"), P(), P())
    return jax.shard_map(
        functools.partial(shards, sizes), mesh=mesh, in_specs=placed,
        out_specs=P("gx", "gy", "gz"), check_vma=False,
    )
```

```python
import functools

import jax
import jax.numpy as jnp
from jax import lax
from jax.experimental import pallas as pl
from jax.experimental.pallas import tpu as pltpu
from jax.sharding import PartitionSpec as P

H = 8
K = 17
ITERS = 2
MESH = pl.DeviceIdType.MESH
F32 = jnp.float32
BF16 = jnp.bfloat16
NOWHERE = -100000
INV_Y = (0, 2, 1)
ROWS = ((0, 128), (128, 64), (192, 64))


def iota(shape, dim):
    return lax.broadcasted_iota(jnp.int32, shape, dim)


def split(value):
    high = value.astype(BF16)
    low = (value - high.astype(F32)).astype(BF16)
    return high, low


def wide(value):
    high, low = split(value)
    return jnp.concatenate([high, low, high], axis=1)


def tall(value):
    high, low = split(value)
    return jnp.concatenate([high, high, low], axis=0)


def z_place(index):
    return jnp.where(
        index < 128 + H,
        index,
        jnp.where(index < 128 + 2 * H, index - 128 - 2 * H, NOWHERE),
    )


def y_place(index):
    return jnp.where(index < 24, index, index - 32)


def pick(offset, tap):
    total = jnp.zeros(offset.shape, F32)
    for t in range(K):
        total = jnp.where(offset == t, tap(t), total)
    return total


def kernel(
    sizes, psf_ref, extents_ref, views_ref, est_ref, out_ref,
    est_in, images, image, forth, back, z_forth, z_back, weights, u_ref, z_ref, z_own, s_ref, sz_ref,
    rc_ref, rz_ref, zc_ref, rz2_ref, est_sem, view_send, view_recv, send, recv, z_send, z_recv,
):
    n_gx, n_gy, n_gz = sizes
    V = image.shape[0]
    gx, gy, gz = lax.axis_index("gx"), lax.axis_index("gy"), lax.axis_index("gz")
    if n_gx == 2:
        x_targets = (gx, 1 - gx)
        x_exists = (None, None)
        x_offset = (0, H - 2 * H * gx)
        inv_x = (0, 1)
    else:
        x_targets = (gx, gx + 1, gx - 1)
        x_exists = (None, gx < n_gx - 1, gx > 0)
        x_offset = (0, H, -H)
        inv_x = (0, 2, 1)
    slots = len(x_targets)
    y_targets = (gy, gy + 1, gy - 1)
    y_exists = (None, gy < n_gy - 1, gy > 0)
    z_targets = (gz + 1, gz - 1)
    z_exists = (gz < n_gz - 1, gz > 0)
    near = []
    for s in range(slots):
        for y in range(3):
            if s == 0 and y == 0:
                continue
            exists = x_exists[s]
            if y_exists[y] is not None:
                exists = y_exists[y] if exists is None else exists & y_exists[y]
            near.append((s, y, exists, {"gx": x_targets[s], "gy": y_targets[y], "gz": gz}))
    started = []

    def under(exists, do):
        if exists is None:
            do()
        else:
            pl.when(exists)(do)

    def start(exists, make):
        under(exists, lambda: make().start())
        started.append((exists, make))

    def remote(src, dst, s_sem, r_sem, device):
        return lambda: pltpu.make_async_remote_copy(
            src_ref=src, dst_ref=dst, send_sem=s_sem, recv_sem=r_sem,
            device_id=device, device_id_type=MESH,
        )

    est_copy = pltpu.make_async_copy(est_ref, est_in, est_sem)
    est_copy.start()
    barrier = pltpu.get_barrier_semaphore()
    expected = jnp.int32(n_gz - 1)
    for k in range(1, n_gz):
        pl.semaphore_signal(
            barrier, inc=1, device_id={"gx": gx, "gy": gy, "gz": lax.rem(gz + k, n_gz)},
            device_id_type=MESH,
        )
    for s, y, exists, device in near:
        under(exists, functools.partial(
            pl.semaphore_signal, barrier, inc=1, device_id=device, device_id_type=MESH))
        expected = expected + (1 if exists is None else exists.astype(jnp.int32))

    own_views = pltpu.make_async_copy(
        views_ref.at[:, :, :, pl.ds(pl.multiple_of(gz * 128, 128), 128)],
        images.at[gz], view_recv.at[0],
    )
    own_views.start()

    def zero_z(side):
        for it in range(ITERS):
            first = 8 * side
            z_ref[it, 0, 0, first:first + 8, :] = jnp.zeros((8, 128), F32)
            rz2_ref[it, 8 - first:16 - first, :] = jnp.zeros((8, 128), F32)

    for side in range(2):
        pl.when(jnp.logical_not(z_exists[side]))(functools.partial(zero_z, side))

    def zero_near(s, y):
        first, count = ROWS[y]
        for it in range(ITERS):
            u_ref[it, s, first:first + count, :] = jnp.zeros((count, 128), F32)
            z_ref[it, s, y] = jnp.zeros((16, 128), F32)
            rc_ref[it, s, y, 0:count, :] = jnp.zeros((count, 128), F32)
            rz_ref[it, s, y] = jnp.zeros((16, 128), F32)

    for s, y, exists, device in near:
        if exists is not None:
            pl.when(jnp.logical_not(exists))(functools.partial(zero_near, s, y))

    est_copy.wait()
    for y in range(16):
        u_ref[0, 0, 8 * y:8 * y + 8, :] = est_in[:, y, :]
    estimate = u_ref[0, 0, 0:128, :]

    def send_estimate(it, value):
        turned = value.T
        z_own[it, 0:8, :] = turned[0:8]
        z_own[it, 8:16, :] = turned[120:128]
        if it == 0:
            pl.semaphore_wait(barrier, expected)
        for side in (0, 1):
            rows = pl.ds(8 - 8 * side, 8)
            start(z_exists[side], remote(
                z_own.at[it, rows], z_ref.at[it, 0, 0, rows],
                z_send.at[it, 0, side], z_recv.at[it, 0, 1 - side],
                {"gx": gx, "gy": gy, "gz": z_targets[side]}))
        for s, y, exists, device in near:
            source = (0, 64, 0)[y]
            first, count = ROWS[INV_Y[y]]
            start(exists, remote(
                u_ref.at[it, 0, pl.ds(source, count)],
                u_ref.at[it, inv_x[s], pl.ds(first, count)],
                send.at[it, 0, 0, s, y], recv.at[it, 0, 0, inv_x[s], INV_Y[y]], device))

    def pass_z(it):
        for side in (0, 1):
            rows = pl.ds(8 * side, 8)
            under(z_exists[side], lambda rows=rows, side=side: remote(
                z_own.at[it, rows], z_ref.at[it, 0, 0, rows],
                z_send.at[it, 0, side], z_recv.at[it, 0, side],
                {"gx": gx, "gy": gy, "gz": z_targets[side]})().wait_recv())
        for s, y, exists, device in near:
            start(exists, remote(
                z_ref.at[it, 0, 0], z_ref.at[it, inv_x[s], INV_Y[y]],
                send.at[it, 0, 1, s, y], recv.at[it, 0, 1, inv_x[s], INV_Y[y]], device))

    send_estimate(0, estimate)
    for k in range(1, n_gz):
        target = lax.rem(gz + k, n_gz)
        start(None, remote(
            views_ref.at[:, :, :, pl.ds(pl.multiple_of(target * 128, 128), 128)],
            images.at[gz], view_send.at[k], view_recv.at[k],
            {"gx": gx, "gy": gy, "gz": target}))

    def build(v, unused):
        def taps(axis):
            return lambda t: psf_ref[v, axis, t]

        scale = jnp.float32(1.0)
        for axis in range(3):
            total = psf_ref[v, axis, 0]
            for t in range(1, K):
                total = total + psf_ref[v, axis, t]
            scale = scale * total
        inverse = 1.0 / jnp.full((8, 128), scale, F32)
        z_band = pick(z_place(iota((144, 128), 0)) - iota((144, 128), 1) + H, taps(2))
        z_band = z_band * inverse[0:1]
        z_band = jnp.concatenate([z_band, jnp.zeros((112, 128), F32)], axis=0)
        z_forth[v] = tall(z_band)
        z_band_t = jnp.concatenate([z_band[0:128].T, z_band[128:256].T], axis=1)
        z_back[v] = tall(z_band_t)
        own = pl.ds(pl.multiple_of(v * 128, 128), 128)
        lane = iota((16, 256), 1)
        y_rows = pick(y_place(lane // 8) - iota((16, 256), 0) + H, taps(1))
        y_rows_t = pick(y_place(iota((32, 128), 0)) - iota((32, 128), 1) // 8 + H, taps(1))
        row = iota((8, 128), 0)
        column = iota((8, 128), 1) % 8
        for s in range(slots):
            x_tile = pick(x_offset[s] + column - row + H, taps(0))
            x_tile_t = pick(x_offset[s] + row - column + H, taps(0))
            for group in range(2):
                block = y_rows[:, None, 128 * group:128 * group + 128] * x_tile[None]
                high, low = split(block.reshape(128, 128))
                first = s * 256 + group * 128
                width = slots * 256
                forth[own, first:first + 128] = high
                forth[own, width + first:width + first + 128] = low
                forth[own, 2 * width + first:2 * width + first + 128] = high
                block = y_rows_t[16 * group:16 * group + 16, None, :] * x_tile_t[None]
                high, low = split(block.reshape(128, 128))
                back[v, first:first + 128, 0:128] = high
                back[v, first:first + 128, 128:256] = low
                back[v, first:first + 128, 256:384] = high
        z_abs = gz * 128 + z_place(iota((8, 256), 1))
        in_z = (z_abs >= extents_ref[v, 2, 0]) & (z_abs < extents_ref[v, 2, 1])
        z_part = jnp.where(in_z, F32(0.75), F32(0.0))[0:1]
        for s in range(slots):
            rows = iota((256, 128), 0)
            y_abs = gy * 16 + y_place(rows // 8)
            x_abs = gx * 8 + x_offset[s] + rows % 8
            inside = (y_abs >= extents_ref[v, 1, 0]) & (y_abs < extents_ref[v, 1, 1])
            inside = inside & (x_abs >= extents_ref[v, 0, 0]) & (x_abs < extents_ref[v, 0, 1])
            flag = jnp.where(inside, F32(1.0), F32(0.0))
            weights[v, s * 256:s * 256 + 256, 0:128] = flag * z_part[:, 0:128] + 0.25
            weights[v, s * 256:s * 256 + 256, 128:256] = flag * z_part[:, 128:256] + 0.25
        return unused

    lax.fori_loop(0, 2, build, 0)
    pass_z(0)
    lax.fori_loop(2, V, build, 0)
    weight_sum = weights[0, 0:128, 0:128]
    for v in range(1, V):
        weight_sum = weight_sum + weights[v, 0:128, 0:128]

    half = iota((16, 128), 1) < 64
    for it in range(ITERS):
        for s, y, exists, device in near:
            first, count = ROWS[y]
            under(exists, lambda s=s, y=y, first=first, count=count, device=device: remote(
                u_ref.at[it, s, pl.ds(first, count)], u_ref.at[it, s, pl.ds(first, count)],
                send.at[it, 0, 0, s, y], recv.at[it, 0, 0, s, y], device)().wait_recv())
        for s, y, exists, device in near:
            under(exists, lambda s=s, y=y, device=device: remote(
                z_ref.at[it, s, y], z_ref.at[it, s, y],
                send.at[it, 0, 1, s, y], recv.at[it, 0, 1, s, y], device)().wait_recv())
        pieces = []
        fill = jnp.zeros((112, 128), F32)
        for s in range(slots):
            halo = jnp.where(half, z_ref[it, s, 1], z_ref[it, s, 2])
            for group, strip in enumerate((z_ref[it, s, 0], halo)):
                turned = jnp.concatenate([strip, fill], axis=0).T
                middle = u_ref[it, s, 128 * group:128 * group + 128, :]
                pieces.append(jnp.concatenate([middle, turned], axis=1))
        padded = tall(jnp.concatenate(pieces, axis=0))
        blurred = []
        across = jnp.dot(forth[...], padded, preferred_element_type=F32)
        for v in range(V):
            lines = wide(across[128 * v:128 * v + 128])
            blurred.append(jnp.dot(lines, z_forth[v], preferred_element_type=F32))
        if it == 0:
            own_views.wait()
            for k in range(1, n_gz):
                remote(
                    images.at[0], images.at[lax.rem(gz + n_gz - k, n_gz)],
                    view_send.at[k], view_recv.at[k],
                    {"gx": gx, "gy": gy, "gz": lax.rem(gz + n_gz - k, n_gz)})().wait_recv()
            per = 16 // n_gz
            for v in range(V):
                for g in range(n_gz):
                    for yy in range(per):
                        first = 8 * (per * g + yy)
                        image[v, first:first + 8, :] = images[g, v, :, yy, :]
        spread = []
        for v in range(V):
            ratio = image[v] / blurred[v]
            lines = jnp.dot(wide(ratio), z_back[v], preferred_element_type=F32)
            spread.append(tall(lines))

        def summed(first):
            total = None
            for v in range(V):
                part = jnp.dot(
                    back[v, first:first + 256, :], spread[v], preferred_element_type=F32)
                part = part * weights[v, first:first + 256, :]
                total = part if total is None else total + part
            return total

        for s in range(slots - 1, -1, -1):
            both = summed(s * 256)
            for group in (1, 0):
                total = both[128 * group:128 * group + 128]
                if s == 0 and group == 0:
                    own_total = total[:, 0:128]
                    own_z = total[:, 128:256].T[0:16]
                    continue
                s_ref[it, s, 128 * group:128 * group + 128, :] = total[:, 0:128]
                sz_ref[it, s, group] = total[:, 128:256].T[0:16]
                for t, y, exists, device in near:
                    if t != s or (y > 0) != (group == 1):
                        continue
                    first, count = ROWS[y]
                    start(exists, remote(
                        sz_ref.at[it, s, group], rz_ref.at[it, inv_x[s], INV_Y[y]],
                        send.at[it, 1, 1, s, y], recv.at[it, 1, 1, inv_x[s], INV_Y[y]], device))
                    start(exists, remote(
                        s_ref.at[it, s, pl.ds(first, count)],
                        rc_ref.at[it, inv_x[s], INV_Y[y], pl.ds(0, count)],
                        send.at[it, 1, 0, s, y], recv.at[it, 1, 0, inv_x[s], INV_Y[y]], device))
        for s, y, exists, device in near:
            under(exists, lambda s=s, y=y, device=device: remote(
                rz_ref.at[it, s, y], rz_ref.at[it, s, y],
                send.at[it, 1, 1, s, y], recv.at[it, 1, 1, s, y], device)().wait_recv())
        for s in range(slots):
            if s > 0:
                own_z = own_z + rz_ref[it, s, 0]
            own_z = own_z + jnp.where(half, rz_ref[it, s, 2], rz_ref[it, s, 1])
        zc_ref[it] = own_z
        for side in (0, 1):
            rows = pl.ds(8 * side, 8)
            start(z_exists[side], remote(
                zc_ref.at[it, rows], rz2_ref.at[it, rows],
                z_send.at[it, 1, side], z_recv.at[it, 1, side],
                {"gx": gx, "gy": gy, "gz": z_targets[side]}))
        for s, y, exists, device in near:
            count = ROWS[y][1]
            under(exists, lambda s=s, y=y, count=count, device=device: remote(
                rc_ref.at[it, s, y, pl.ds(0, count)], rc_ref.at[it, s, y, pl.ds(0, count)],
                send.at[it, 1, 0, s, y], recv.at[it, 1, 0, s, y], device)().wait_recv())
        for s in range(slots):
            if s > 0:
                own_total = own_total + rc_ref[it, s, 0]
            own_total = own_total + jnp.concatenate(
                [rc_ref[it, s, 2, 0:64, :], rc_ref[it, s, 1, 0:64, :]], axis=0)
        for side in (0, 1):
            rows = pl.ds(8 * side, 8)
            under(z_exists[1 - side], lambda rows=rows, side=side: remote(
                zc_ref.at[it, rows], rz2_ref.at[it, rows],
                z_send.at[it, 1, side], z_recv.at[it, 1, side],
                {"gx": gx, "gy": gy, "gz": z_targets[1 - side]})().wait_recv())
        edge = jnp.concatenate(
            [rz2_ref[it, 0:8, :], jnp.zeros((112, 128), F32), rz2_ref[it, 8:16, :]], axis=0)
        own_total = own_total + edge.T
        estimate = estimate * (own_total / weight_sum)
        if it < ITERS - 1:
            u_ref[it + 1, 0, 0:128, :] = estimate
            send_estimate(it + 1, estimate)
            pass_z(it + 1)
    for y in range(16):
        out_ref[:, y, :] = estimate[8 * y:8 * y + 8, :]
    for exists, make in started:
        under(exists, lambda make=make: make().wait_send())


def shards(sizes, views, estimate, psf, extents):
    n_gx, n_gy, n_gz = sizes
    V = views.shape[0]
    slots = 2 if n_gx == 2 else 3
    rows = slots * 256
    smem = pl.BlockSpec(memory_space=pltpu.SMEM)
    vmem = pl.BlockSpec(memory_space=pltpu.VMEM)
    whole = pl.BlockSpec(memory_space=pl.ANY)
    return pl.pallas_call(
        functools.partial(kernel, sizes),
        out_shape=jax.ShapeDtypeStruct(estimate.shape, F32),
        in_specs=[smem, smem, whole, whole],
        out_specs=vmem,
        scratch_shapes=[
            pltpu.VMEM(estimate.shape, F32),
            pltpu.VMEM((n_gz,) + views.shape[:3] + (128,), F32),
            pltpu.VMEM((V, 128, 128), F32),
            pltpu.VMEM((V * 128, 3 * rows), BF16),
            pltpu.VMEM((V, rows, 384), BF16),
            pltpu.VMEM((V, 768, 128), BF16),
            pltpu.VMEM((V, 384, 256), BF16),
            pltpu.VMEM((V, rows, 256), F32),
            pltpu.VMEM((ITERS, slots, 256, 128), F32),
            pltpu.VMEM((ITERS, slots, 3, 16, 128), F32),
            pltpu.VMEM((ITERS, 16, 128), F32),
            pltpu.VMEM((ITERS, slots, 256, 128), F32),
            pltpu.VMEM((ITERS, slots, 2, 16, 128), F32),
            pltpu.VMEM((ITERS, slots, 3, 128, 128), F32),
            pltpu.VMEM((ITERS, slots, 3, 16, 128), F32),
            pltpu.VMEM((ITERS, 16, 128), F32),
            pltpu.VMEM((ITERS, 16, 128), F32),
            pltpu.SemaphoreType.DMA,
            pltpu.SemaphoreType.DMA((n_gz,)),
            pltpu.SemaphoreType.DMA((n_gz,)),
            pltpu.SemaphoreType.DMA((ITERS, 2, 2, slots, 3)),
            pltpu.SemaphoreType.DMA((ITERS, 2, 2, slots, 3)),
            pltpu.SemaphoreType.DMA((ITERS, 2, 2)),
            pltpu.SemaphoreType.DMA((ITERS, 2, 2)),
        ],
        compiler_params=pltpu.CompilerParams(
            collective_id=0, has_side_effects=True, vmem_limit_bytes=60 * 1024 * 1024
        ),
    )(psf, extents, views, estimate)


def solution(mesh):
    sizes = (mesh.shape["gx"], mesh.shape["gy"], mesh.shape["gz"])
    placed = (P(None, "gx", ("gy", "gz"), None), P("gx", "gy", "gz"), P(), P())
    return jax.shard_map(
        functools.partial(shards, sizes), mesh=mesh, in_specs=placed,
        out_specs=P("gx", "gy", "gz"), check_vma=False,
    )
```

```python
import functools

import jax
import jax.numpy as jnp
from jax import lax
from jax.experimental import pallas as pl
from jax.experimental.pallas import tpu as pltpu
from jax.sharding import PartitionSpec as P

H = 8
K = 17
ITERS = 2
MESH = pl.DeviceIdType.MESH
F32 = jnp.float32
BF16 = jnp.bfloat16
NOWHERE = -100000
INV_Y = (0, 2, 1)
ROWS = ((0, 128), (128, 64), (192, 64))


def iota(shape, dim):
    return lax.broadcasted_iota(jnp.int32, shape, dim)


def split(value):
    high = value.astype(BF16)
    low = (value - high.astype(F32)).astype(BF16)
    return high, low


def wide(value):
    high, low = split(value)
    return jnp.concatenate([high, low, high], axis=1)


def tall(value):
    high, low = split(value)
    return jnp.concatenate([high, high, low], axis=0)


def z_place(index):
    return jnp.where(
        index < 128 + H,
        index,
        jnp.where(index < 128 + 2 * H, index - 128 - 2 * H, NOWHERE),
    )


def y_place(index):
    return jnp.where(index < 24, index, index - 32)


def pick(offset, tap):
    total = jnp.zeros(offset.shape, F32)
    for t in range(K):
        total = jnp.where(offset == t, tap(t), total)
    return total


def kernel(
    sizes, psf_ref, extents_ref, views_ref, est_ref, out_ref,
    est_in, images, image, forth, back, z_forth, z_back, weights, u_ref, z_ref, z_own, s_ref, sz_ref,
    rc_ref, rz_ref, est_sem, view_send, view_recv, send, recv, z_send, z_recv,
):
    n_gx, n_gy, n_gz = sizes
    V = image.shape[0]
    gx, gy, gz = lax.axis_index("gx"), lax.axis_index("gy"), lax.axis_index("gz")
    if n_gx == 2:
        x_targets = (gx, 1 - gx)
        x_exists = (None, None)
        x_offset = (0, H - 2 * H * gx)
        inv_x = (0, 1)
    else:
        x_targets = (gx, gx + 1, gx - 1)
        x_exists = (None, gx < n_gx - 1, gx > 0)
        x_offset = (0, H, -H)
        inv_x = (0, 2, 1)
    slots = len(x_targets)
    y_targets = (gy, gy + 1, gy - 1)
    y_exists = (None, gy < n_gy - 1, gy > 0)
    z_targets = (gz + 1, gz - 1)
    z_exists = (gz < n_gz - 1, gz > 0)
    near = []
    for s in range(slots):
        for y in range(3):
            if s == 0 and y == 0:
                continue
            exists = x_exists[s]
            if y_exists[y] is not None:
                exists = y_exists[y] if exists is None else exists & y_exists[y]
            near.append((s, y, exists, {"gx": x_targets[s], "gy": y_targets[y], "gz": gz}))
    side_near = []
    for s in range(slots):
        for y in range(3):
            for side in range(2):
                exists = z_exists[side]
                for other in (x_exists[s], y_exists[y]):
                    if other is not None:
                        exists = exists & other
                device = {"gx": x_targets[s], "gy": y_targets[y], "gz": z_targets[side]}
                side_near.append((s, y, side, exists, device))
    started = []

    def under(exists, do):
        if exists is None:
            do()
        else:
            pl.when(exists)(do)

    def start(exists, make):
        under(exists, lambda: make().start())
        started.append((exists, make))

    def remote(src, dst, s_sem, r_sem, device):
        return lambda: pltpu.make_async_remote_copy(
            src_ref=src, dst_ref=dst, send_sem=s_sem, recv_sem=r_sem,
            device_id=device, device_id_type=MESH,
        )

    est_copy = pltpu.make_async_copy(est_ref, est_in, est_sem)
    est_copy.start()
    barrier = pltpu.get_barrier_semaphore()
    expected = jnp.int32(n_gz - 1)
    for s, y, side, exists, device in side_near:
        if s == 0 and y == 0:
            continue
        under(exists, functools.partial(
            pl.semaphore_signal, barrier, inc=1, device_id=device, device_id_type=MESH))
        expected = expected + exists.astype(jnp.int32)
    for k in range(1, n_gz):
        pl.semaphore_signal(
            barrier, inc=1, device_id={"gx": gx, "gy": gy, "gz": lax.rem(gz + k, n_gz)},
            device_id_type=MESH,
        )
    for s, y, exists, device in near:
        under(exists, functools.partial(
            pl.semaphore_signal, barrier, inc=1, device_id=device, device_id_type=MESH))
        expected = expected + (1 if exists is None else exists.astype(jnp.int32))

    own_views = pltpu.make_async_copy(
        views_ref.at[:, :, :, pl.ds(pl.multiple_of(gz * 128, 128), 128)],
        images.at[gz], view_recv.at[0],
    )
    own_views.start()

    def zero_side(s, y, side):
        first = 8 * side
        for it in range(ITERS):
            z_ref[it, s, y, first:first + 8, :] = jnp.zeros((8, 128), F32)
            rz_ref[it, s, y, 8 - first:16 - first, :] = jnp.zeros((8, 128), F32)

    for s, y, side, exists, device in side_near:
        pl.when(jnp.logical_not(exists))(functools.partial(zero_side, s, y, side))

    def zero_near(s, y):
        first, count = ROWS[y]
        for it in range(ITERS):
            u_ref[it, s, first:first + count, :] = jnp.zeros((count, 128), F32)
            rc_ref[it, s, y, 0:count, :] = jnp.zeros((count, 128), F32)

    for s, y, exists, device in near:
        if exists is not None:
            pl.when(jnp.logical_not(exists))(functools.partial(zero_near, s, y))

    est_copy.wait()
    for y in range(16):
        u_ref[0, 0, 8 * y:8 * y + 8, :] = est_in[:, y, :]
    estimate = u_ref[0, 0, 0:128, :]

    def send_estimate(it, value):
        if it == 0:
            pl.semaphore_wait(barrier, expected)
        for s, y, exists, device in near[::-1]:
            source = (0, 64, 0)[y]
            first, count = ROWS[INV_Y[y]]
            start(exists, remote(
                u_ref.at[it, 0, pl.ds(source, count)],
                u_ref.at[it, inv_x[s], pl.ds(first, count)],
                send.at[it, 0, s, y], recv.at[it, 0, inv_x[s], INV_Y[y]], device))
        turned = value.T
        z_own[it, 0:8, :] = turned[0:8]
        z_own[it, 8:16, :] = turned[120:128]
        for s, y, side, exists, device in side_near[::-1]:
            rows = pl.ds(8 - 8 * side, 8)
            start(exists, remote(
                z_own.at[it, rows], z_ref.at[it, inv_x[s], INV_Y[y], rows],
                z_send.at[it, 0, s, y, side], z_recv.at[it, 0, inv_x[s], INV_Y[y], 1 - side],
                device))

    send_estimate(0, estimate)
    for k in range(1, n_gz):
        target = lax.rem(gz + k, n_gz)
        start(None, remote(
            views_ref.at[:, :, :, pl.ds(pl.multiple_of(target * 128, 128), 128)],
            images.at[gz], view_send.at[k], view_recv.at[k],
            {"gx": gx, "gy": gy, "gz": target}))

    def build(v, unused):
        def taps(axis):
            return lambda t: psf_ref[v, axis, t]

        scale = jnp.float32(1.0)
        for axis in range(3):
            total = psf_ref[v, axis, 0]
            for t in range(1, K):
                total = total + psf_ref[v, axis, t]
            scale = scale * total
        inverse = 1.0 / jnp.full((8, 128), scale, F32)
        z_band = pick(z_place(iota((144, 128), 0)) - iota((144, 128), 1) + H, taps(2))
        z_band = z_band * inverse[0:1]
        z_band = jnp.concatenate([z_band, jnp.zeros((112, 128), F32)], axis=0)
        z_forth[v] = tall(z_band)
        z_band_t = jnp.concatenate([z_band[0:128].T, z_band[128:256].T], axis=1)
        z_back[v] = tall(z_band_t)
        own = pl.ds(pl.multiple_of(v * 128, 128), 128)
        lane = iota((16, 256), 1)
        y_rows = pick(y_place(lane // 8) - iota((16, 256), 0) + H, taps(1))
        y_rows_t = pick(y_place(iota((32, 128), 0)) - iota((32, 128), 1) // 8 + H, taps(1))
        row = iota((8, 128), 0)
        column = iota((8, 128), 1) % 8
        for s in range(slots):
            x_tile = pick(x_offset[s] + column - row + H, taps(0))
            x_tile_t = pick(x_offset[s] + row - column + H, taps(0))
            for group in range(2):
                block = y_rows[:, None, 128 * group:128 * group + 128] * x_tile[None]
                high, low = split(block.reshape(128, 128))
                first = s * 256 + group * 128
                width = slots * 256
                forth[own, first:first + 128] = high
                forth[own, width + first:width + first + 128] = low
                forth[own, 2 * width + first:2 * width + first + 128] = high
                block = y_rows_t[16 * group:16 * group + 16, None, :] * x_tile_t[None]
                high, low = split(block.reshape(128, 128))
                back[v, first:first + 128, 0:128] = high
                back[v, first:first + 128, 128:256] = low
                back[v, first:first + 128, 256:384] = high
        z_abs = gz * 128 + z_place(iota((8, 256), 1))
        in_z = (z_abs >= extents_ref[2, 0, v]) & (z_abs < extents_ref[2, 1, v])
        z_part = jnp.where(in_z, F32(0.75), F32(0.0))[0:1]
        for s in range(slots):
            rows = iota((256, 128), 0)
            y_abs = gy * 16 + y_place(rows // 8)
            x_abs = gx * 8 + x_offset[s] + rows % 8
            inside = (y_abs >= extents_ref[1, 0, v]) & (y_abs < extents_ref[1, 1, v])
            inside = inside & (x_abs >= extents_ref[0, 0, v]) & (x_abs < extents_ref[0, 1, v])
            flag = jnp.where(inside, F32(1.0), F32(0.0))
            weights[v, s * 256:s * 256 + 256, 0:128] = flag * z_part[:, 0:128] + 0.25
            weights[v, s * 256:s * 256 + 256, 128:256] = flag * z_part[:, 128:256] + 0.25
        return unused

    lax.fori_loop(0, V, build, 0)
    weight_sum = weights[0, 0:128, 0:128]
    for v in range(1, V):
        weight_sum = weight_sum + weights[v, 0:128, 0:128]

    half = iota((16, 128), 1) < 64
    for it in range(ITERS):
        for s, y, exists, device in near:
            first, count = ROWS[y]
            under(exists, lambda s=s, y=y, first=first, count=count, device=device: remote(
                u_ref.at[it, s, pl.ds(first, count)], u_ref.at[it, s, pl.ds(first, count)],
                send.at[it, 0, s, y], recv.at[it, 0, s, y], device)().wait_recv())
        for s, y, side, exists, device in side_near:
            rows = pl.ds(8 * side, 8)
            under(exists, lambda s=s, y=y, side=side, rows=rows, device=device: remote(
                z_own.at[it, rows], z_ref.at[it, s, y, rows],
                z_send.at[it, 0, s, y, side], z_recv.at[it, 0, s, y, side], device)().wait_recv())
        pieces = []
        fill = jnp.zeros((112, 128), F32)
        for s in range(slots):
            halo = jnp.where(half, z_ref[it, s, 1], z_ref[it, s, 2])
            for group, strip in enumerate((z_ref[it, s, 0], halo)):
                turned = jnp.concatenate([strip, fill], axis=0).T
                middle = u_ref[it, s, 128 * group:128 * group + 128, :]
                pieces.append(jnp.concatenate([middle, turned], axis=1))
        padded = tall(jnp.concatenate(pieces, axis=0))
        blurred = []
        across = jnp.dot(forth[...], padded, preferred_element_type=F32)
        for v in range(V):
            lines = wide(across[128 * v:128 * v + 128])
            blurred.append(jnp.dot(lines, z_forth[v], preferred_element_type=F32))
        if it == 0:
            own_views.wait()
            for k in range(1, n_gz):
                remote(
                    images.at[0], images.at[lax.rem(gz + n_gz - k, n_gz)],
                    view_send.at[k], view_recv.at[k],
                    {"gx": gx, "gy": gy, "gz": lax.rem(gz + n_gz - k, n_gz)})().wait_recv()
            per = 16 // n_gz
            for v in range(V):
                for g in range(n_gz):
                    for yy in range(per):
                        first = 8 * (per * g + yy)
                        image[v, first:first + 8, :] = images[g, v, :, yy, :]
        spread = []
        for v in range(V):
            ratio = image[v] / blurred[v]
            lines = jnp.dot(wide(ratio), z_back[v], preferred_element_type=F32)
            spread.append(tall(lines))

        def summed(first):
            total = None
            for v in range(V):
                part = jnp.dot(
                    back[v, first:first + 256, :], spread[v], preferred_element_type=F32)
                part = part * weights[v, first:first + 256, :]
                total = part if total is None else total + part
            return total

        for s in range(slots - 1, -1, -1):
            both = summed(s * 256)
            if s == 0:
                own_total = both[0:128, 0:128]
                s_ref[it, s, 128:256, :] = both[128:256, 0:128]
            else:
                s_ref[it, s] = both[:, 0:128]
            for t, y, exists, device in near:
                if t != s:
                    continue
                first, count = ROWS[y]
                start(exists, remote(
                    s_ref.at[it, s, pl.ds(first, count)],
                    rc_ref.at[it, inv_x[s], INV_Y[y], pl.ds(0, count)],
                    send.at[it, 1, s, y], recv.at[it, 1, inv_x[s], INV_Y[y]], device))
            for group in (0, 1):
                sz_ref[it, s, group] = both[128 * group:128 * group + 128, 128:256].T[0:16]
            for t, y, side, exists, device in side_near:
                if t != s:
                    continue
                rows = pl.ds(8 * side, 8)
                start(exists, remote(
                    sz_ref.at[it, s, min(y, 1), rows],
                    rz_ref.at[it, inv_x[s], INV_Y[y], rows],
                    z_send.at[it, 1, s, y, side], z_recv.at[it, 1, inv_x[s], INV_Y[y], 1 - side],
                    device))
        for s, y, side, exists, device in side_near:
            rows = pl.ds(8 - 8 * side, 8)
            under(exists, lambda s=s, y=y, side=side, rows=rows, device=device: remote(
                sz_ref.at[it, s, 0, rows], rz_ref.at[it, s, y, rows],
                z_send.at[it, 1, s, y, side], z_recv.at[it, 1, s, y, side], device)().wait_recv())
        strips = jnp.zeros((16, 128), F32)
        for s in range(slots):
            strips = strips + rz_ref[it, s, 0]
            strips = strips + jnp.where(half, rz_ref[it, s, 2], rz_ref[it, s, 1])
        edge = jnp.concatenate([strips[0:8], jnp.zeros((112, 128), F32), strips[8:16]], axis=0)
        own_total = own_total + edge.T
        for s, y, exists, device in near:
            count = ROWS[y][1]
            under(exists, lambda s=s, y=y, count=count, device=device: remote(
                rc_ref.at[it, s, y, pl.ds(0, count)], rc_ref.at[it, s, y, pl.ds(0, count)],
                send.at[it, 1, s, y], recv.at[it, 1, s, y], device)().wait_recv())
        for s in range(slots):
            if s > 0:
                own_total = own_total + rc_ref[it, s, 0]
            own_total = own_total + jnp.concatenate(
                [rc_ref[it, s, 2, 0:64, :], rc_ref[it, s, 1, 0:64, :]], axis=0)
        estimate = estimate * (own_total / weight_sum)
        if it < ITERS - 1:
            u_ref[it + 1, 0, 0:128, :] = estimate
            send_estimate(it + 1, estimate)
    for y in range(16):
        out_ref[:, y, :] = estimate[8 * y:8 * y + 8, :]
    for exists, make in started:
        under(exists, lambda make=make: make().wait_send())


def shards(sizes, views, estimate, psf, extents):
    n_gx, n_gy, n_gz = sizes
    V = views.shape[0]
    slots = 2 if n_gx == 2 else 3
    rows = slots * 256
    smem = pl.BlockSpec(memory_space=pltpu.SMEM)
    vmem = pl.BlockSpec(memory_space=pltpu.VMEM)
    whole = pl.BlockSpec(memory_space=pltpu.HBM)
    return pl.pallas_call(
        functools.partial(kernel, sizes),
        out_shape=jax.ShapeDtypeStruct(estimate.shape, F32),
        in_specs=[smem, smem, whole, whole],
        out_specs=vmem,
        scratch_shapes=[
            pltpu.VMEM(estimate.shape, F32),
            pltpu.VMEM((n_gz,) + views.shape[:3] + (128,), F32),
            pltpu.VMEM((V, 128, 128), F32),
            pltpu.VMEM((V * 128, 3 * rows), BF16),
            pltpu.VMEM((V, rows, 384), BF16),
            pltpu.VMEM((V, 768, 128), BF16),
            pltpu.VMEM((V, 384, 256), BF16),
            pltpu.VMEM((V, rows, 256), F32),
            pltpu.VMEM((ITERS, slots, 256, 128), F32),
            pltpu.VMEM((ITERS, slots, 3, 16, 128), F32),
            pltpu.VMEM((ITERS, 16, 128), F32),
            pltpu.VMEM((ITERS, slots, 256, 128), F32),
            pltpu.VMEM((ITERS, slots, 2, 16, 128), F32),
            pltpu.VMEM((ITERS, slots, 3, 128, 128), F32),
            pltpu.VMEM((ITERS, slots, 3, 16, 128), F32),
            pltpu.SemaphoreType.DMA,
            pltpu.SemaphoreType.DMA((n_gz,)),
            pltpu.SemaphoreType.DMA((n_gz,)),
            pltpu.SemaphoreType.DMA((ITERS, 2, slots, 3)),
            pltpu.SemaphoreType.DMA((ITERS, 2, slots, 3)),
            pltpu.SemaphoreType.DMA((ITERS, 2, slots, 3, 2)),
            pltpu.SemaphoreType.DMA((ITERS, 2, slots, 3, 2)),
        ],
        compiler_params=pltpu.CompilerParams(
            collective_id=0, has_side_effects=True, vmem_limit_bytes=60 * 1024 * 1024
        ),
    )(psf, extents.transpose(1, 2, 0), views, estimate)


def solution(mesh):
    sizes = (mesh.shape["gx"], mesh.shape["gy"], mesh.shape["gz"])
    placed = (P(None, "gx", ("gy", "gz"), None), P("gx", "gy", "gz"), P(), P())
    return jax.shard_map(
        functools.partial(shards, sizes), mesh=mesh, in_specs=placed,
        out_specs=P("gx", "gy", "gz"), check_vma=False,
    )
```

```python
import functools

import jax
import jax.numpy as jnp
from jax import lax
from jax.experimental import pallas as pl
from jax.experimental.pallas import tpu as pltpu
from jax.sharding import PartitionSpec as P

H = 8
K = 17
ITERS = 2
MESH = pl.DeviceIdType.MESH
F32 = jnp.float32
BF16 = jnp.bfloat16
NOWHERE = -100000
INV_Y = (0, 2, 1)
ROWS = ((0, 128), (128, 64), (192, 64))


def iota(shape, dim):
    return lax.broadcasted_iota(jnp.int32, shape, dim)


def split(value):
    high = value.astype(BF16)
    low = (value - high.astype(F32)).astype(BF16)
    return high, low


def wide(value):
    high, low = split(value)
    return jnp.concatenate([high, low, high], axis=1)


def tall(value):
    high, low = split(value)
    return jnp.concatenate([high, high, low], axis=0)


def z_place(index):
    return jnp.where(
        index < 128 + H,
        index,
        jnp.where(index < 128 + 2 * H, index - 128 - 2 * H, NOWHERE),
    )


def y_place(index):
    return jnp.where(index < 24, index, index - 32)


def pick(offset, tap):
    total = jnp.zeros(offset.shape, F32)
    for t in range(K):
        total = jnp.where(offset == t, tap(t), total)
    return total


def kernel(
    sizes, psf_in, extents_in, views_ref, est_ref, out_ref,
    psf_ref, extents_ref, est_in, images, image, forth, back, z_forth, z_back, weights, u_ref, z_ref, z_own, s_ref, sz_ref,
    rc_ref, rz_ref, est_sem, view_send, view_recv, send, recv, z_send, z_recv,
):
    n_gx, n_gy, n_gz = sizes
    V = image.shape[0]
    gx, gy, gz = lax.axis_index("gx"), lax.axis_index("gy"), lax.axis_index("gz")
    if n_gx == 2:
        x_targets = (gx, 1 - gx)
        x_exists = (None, None)
        x_offset = (0, H - 2 * H * gx)
        inv_x = (0, 1)
    else:
        x_targets = (gx, gx + 1, gx - 1)
        x_exists = (None, gx < n_gx - 1, gx > 0)
        x_offset = (0, H, -H)
        inv_x = (0, 2, 1)
    slots = len(x_targets)
    y_targets = (gy, gy + 1, gy - 1)
    y_exists = (None, gy < n_gy - 1, gy > 0)
    z_targets = (gz + 1, gz - 1)
    z_exists = (gz < n_gz - 1, gz > 0)
    near = []
    for s in range(slots):
        for y in range(3):
            if s == 0 and y == 0:
                continue
            exists = x_exists[s]
            if y_exists[y] is not None:
                exists = y_exists[y] if exists is None else exists & y_exists[y]
            near.append((s, y, exists, {"gx": x_targets[s], "gy": y_targets[y], "gz": gz}))
    side_near = []
    for s in range(slots):
        for y in range(3):
            for side in range(2):
                exists = z_exists[side]
                for other in (x_exists[s], y_exists[y]):
                    if other is not None:
                        exists = exists & other
                device = {"gx": x_targets[s], "gy": y_targets[y], "gz": z_targets[side]}
                side_near.append((s, y, side, exists, device))
    started = []

    def under(exists, do):
        if exists is None:
            do()
        else:
            pl.when(exists)(do)

    def start(exists, make):
        under(exists, lambda: make().start())
        started.append((exists, make))

    def drain():
        for exists, make in started:
            under(exists, lambda make=make: make().wait_send())
        started.clear()

    def remote(src, dst, s_sem, r_sem, device):
        return lambda: pltpu.make_async_remote_copy(
            src_ref=src, dst_ref=dst, send_sem=s_sem, recv_sem=r_sem,
            device_id=device, device_id_type=MESH,
        )

    est_copy = pltpu.make_async_copy(est_ref, est_in, est_sem.at[0])
    psf_copy = pltpu.make_async_copy(psf_in, psf_ref, est_sem.at[1])
    extents_copy = pltpu.make_async_copy(extents_in, extents_ref, est_sem.at[2])
    est_copy.start()
    barrier = pltpu.get_barrier_semaphore()
    expected = jnp.int32(n_gz - 1)
    for s, y, side, exists, device in side_near:
        if s == 0 and y == 0:
            continue
        under(exists, functools.partial(
            pl.semaphore_signal, barrier, inc=1, device_id=device, device_id_type=MESH))
        expected = expected + exists.astype(jnp.int32)
    for k in range(1, n_gz):
        pl.semaphore_signal(
            barrier, inc=1, device_id={"gx": gx, "gy": gy, "gz": lax.rem(gz + k, n_gz)},
            device_id_type=MESH,
        )
    for s, y, exists, device in near:
        under(exists, functools.partial(
            pl.semaphore_signal, barrier, inc=1, device_id=device, device_id_type=MESH))
        expected = expected + (1 if exists is None else exists.astype(jnp.int32))

    psf_copy.start()
    extents_copy.start()
    own_views = pltpu.make_async_copy(
        views_ref.at[:, :, :, pl.ds(pl.multiple_of(gz * 128, 128), 128)],
        images.at[gz], view_recv.at[0],
    )
    own_views.start()

    def zero_side(s, y, side):
        first = 8 * side
        for it in range(ITERS):
            z_ref[it, s, y, first:first + 8, :] = jnp.zeros((8, 128), F32)
            rz_ref[it, s, y, 8 - first:16 - first, :] = jnp.zeros((8, 128), F32)

    for s, y, side, exists, device in side_near:
        pl.when(jnp.logical_not(exists))(functools.partial(zero_side, s, y, side))

    def zero_near(s, y):
        first, count = ROWS[y]
        for it in range(ITERS):
            u_ref[it, s, first:first + count, :] = jnp.zeros((count, 128), F32)
            rc_ref[it, s, y, 0:count, :] = jnp.zeros((count, 128), F32)

    for s, y, exists, device in near:
        if exists is not None:
            pl.when(jnp.logical_not(exists))(functools.partial(zero_near, s, y))

    est_copy.wait()
    for y in range(16):
        u_ref[0, 0, 8 * y:8 * y + 8, :] = est_in[:, y, :]
    estimate = u_ref[0, 0, 0:128, :]

    def send_estimate(it, value):
        if it == 0:
            pl.semaphore_wait(barrier, expected)
        for s, y, exists, device in near[::-1]:
            source = (0, 64, 0)[y]
            first, count = ROWS[INV_Y[y]]
            start(exists, remote(
                u_ref.at[it, 0, pl.ds(source, count)],
                u_ref.at[it, inv_x[s], pl.ds(first, count)],
                send.at[it, 0, s, y], recv.at[it, 0, inv_x[s], INV_Y[y]], device))
        turned = value.T
        z_own[it, 0:8, :] = turned[0:8]
        z_own[it, 8:16, :] = turned[120:128]
        for s, y, side, exists, device in side_near[::-1]:
            rows = pl.ds(8 - 8 * side, 8)
            start(exists, remote(
                z_own.at[it, rows], z_ref.at[it, inv_x[s], INV_Y[y], rows],
                z_send.at[it, 0, s, y, side], z_recv.at[it, 0, inv_x[s], INV_Y[y], 1 - side],
                device))

    send_estimate(0, estimate)
    halo_sends = list(started)
    started.clear()
    for k in range(1, n_gz):
        target = lax.rem(gz + k, n_gz)
        start(None, remote(
            views_ref.at[:, :, :, pl.ds(pl.multiple_of(target * 128, 128), 128)],
            images.at[gz], view_send.at[k], view_recv.at[k],
            {"gx": gx, "gy": gy, "gz": target}))

    view_sends = list(started)
    started[:] = halo_sends

    def build(v, unused):
        def taps(axis):
            return lambda t: psf_ref[v, axis, t]

        scale = jnp.float32(1.0)
        for axis in range(3):
            total = psf_ref[v, axis, 0]
            for t in range(1, K):
                total = total + psf_ref[v, axis, t]
            scale = scale * total
        inverse = 1.0 / jnp.full((8, 128), scale, F32)
        z_band = pick(z_place(iota((144, 128), 0)) - iota((144, 128), 1) + H, taps(2))
        z_band = z_band * inverse[0:1]
        z_band = jnp.concatenate([z_band, jnp.zeros((112, 128), F32)], axis=0)
        z_forth[v] = tall(z_band)
        z_band_t = jnp.concatenate([z_band[0:128].T, z_band[128:256].T], axis=1)
        z_back[v] = tall(z_band_t)
        own = pl.ds(pl.multiple_of(v * 128, 128), 128)
        lane = iota((16, 256), 1)
        y_rows = pick(y_place(lane // 8) - iota((16, 256), 0) + H, taps(1))
        y_rows_t = pick(y_place(iota((32, 128), 0)) - iota((32, 128), 1) // 8 + H, taps(1))
        row = iota((8, 128), 0)
        column = iota((8, 128), 1) % 8
        for s in range(slots):
            x_tile = pick(x_offset[s] + column - row + H, taps(0))
            x_tile_t = pick(x_offset[s] + row - column + H, taps(0))
            for group in range(2):
                block = y_rows[:, None, 128 * group:128 * group + 128] * x_tile[None]
                high, low = split(block.reshape(128, 128))
                first = s * 256 + group * 128
                width = slots * 256
                forth[own, first:first + 128] = high
                forth[own, width + first:width + first + 128] = low
                forth[own, 2 * width + first:2 * width + first + 128] = high
                block = y_rows_t[16 * group:16 * group + 16, None, :] * x_tile_t[None]
                high, low = split(block.reshape(128, 128))
                back[v, first:first + 128, 0:128] = high
                back[v, first:first + 128, 128:256] = low
                back[v, first:first + 128, 256:384] = high
        z_abs = gz * 128 + z_place(iota((8, 256), 1))
        in_z = (z_abs >= extents_ref[2, 0, v]) & (z_abs < extents_ref[2, 1, v])
        z_part = jnp.where(in_z, F32(0.75), F32(0.0))[0:1]
        for s in range(slots):
            rows = iota((256, 128), 0)
            y_abs = gy * 16 + y_place(rows // 8)
            x_abs = gx * 8 + x_offset[s] + rows % 8
            inside = (y_abs >= extents_ref[1, 0, v]) & (y_abs < extents_ref[1, 1, v])
            inside = inside & (x_abs >= extents_ref[0, 0, v]) & (x_abs < extents_ref[0, 1, v])
            flag = jnp.where(inside, F32(1.0), F32(0.0))
            weights[v, s * 256:s * 256 + 256, 0:128] = flag * z_part[:, 0:128] + 0.25
            weights[v, s * 256:s * 256 + 256, 128:256] = flag * z_part[:, 128:256] + 0.25
        return unused

    psf_copy.wait()
    extents_copy.wait()

    def build_pair(i, unused):
        return build(2 * i + 1, build(2 * i, unused))

    lax.fori_loop(0, V // 2, build_pair, 0)
    if V % 2:
        build(V - 1, 0)
    weight_sum = weights[0, 0:128, 0:128]
    for v in range(1, V):
        weight_sum = weight_sum + weights[v, 0:128, 0:128]

    half = iota((16, 128), 1) < 64
    for it in range(ITERS):
        drain()
        for s, y, exists, device in near:
            first, count = ROWS[y]
            under(exists, lambda s=s, y=y, first=first, count=count, device=device: remote(
                u_ref.at[it, s, pl.ds(first, count)], u_ref.at[it, s, pl.ds(first, count)],
                send.at[it, 0, s, y], recv.at[it, 0, s, y], device)().wait_recv())
        for s, y, side, exists, device in side_near:
            rows = pl.ds(8 * side, 8)
            under(exists, lambda s=s, y=y, side=side, rows=rows, device=device: remote(
                z_own.at[it, rows], z_ref.at[it, s, y, rows],
                z_send.at[it, 0, s, y, side], z_recv.at[it, 0, s, y, side], device)().wait_recv())
        pieces = []
        fill = jnp.zeros((112, 128), F32)
        for s in range(slots):
            halo = jnp.where(half, z_ref[it, s, 1], z_ref[it, s, 2])
            for group, strip in enumerate((z_ref[it, s, 0], halo)):
                turned = jnp.concatenate([strip, fill], axis=0).T
                middle = u_ref[it, s, 128 * group:128 * group + 128, :]
                pieces.append(jnp.concatenate([middle, turned], axis=1))
        padded = tall(jnp.concatenate(pieces, axis=0))
        blurred = []
        across = jnp.dot(forth[...], padded, preferred_element_type=F32)
        for v in range(V):
            lines = wide(across[128 * v:128 * v + 128])
            blurred.append(jnp.dot(lines, z_forth[v], preferred_element_type=F32))
        if it == 0:
            own_views.wait()
            for k in range(1, n_gz):
                remote(
                    images.at[0], images.at[lax.rem(gz + n_gz - k, n_gz)],
                    view_send.at[k], view_recv.at[k],
                    {"gx": gx, "gy": gy, "gz": lax.rem(gz + n_gz - k, n_gz)})().wait_recv()
            per = 16 // n_gz
            for v in range(V):
                for g in range(n_gz):
                    for yy in range(per):
                        first = 8 * (per * g + yy)
                        image[v, first:first + 8, :] = images[g, v, :, yy, :]
        spread = []
        for v in range(V):
            ratio = image[v] / blurred[v]
            lines = jnp.dot(wide(ratio), z_back[v], preferred_element_type=F32)
            spread.append(tall(lines))

        def summed(first):
            total = None
            for v in range(V):
                part = jnp.dot(
                    back[v, first:first + 256, :], spread[v], preferred_element_type=F32)
                part = part * weights[v, first:first + 256, :]
                total = part if total is None else total + part
            return total

        for s in range(slots - 1, -1, -1):
            both = summed(s * 256)
            if s == 0:
                own_total = both[0:128, 0:128]
                s_ref[it, s, 128:256, :] = both[128:256, 0:128]
            else:
                s_ref[it, s] = both[:, 0:128]
            for t, y, exists, device in near:
                if t != s:
                    continue
                first, count = ROWS[y]
                start(exists, remote(
                    s_ref.at[it, s, pl.ds(first, count)],
                    rc_ref.at[it, inv_x[s], INV_Y[y], pl.ds(0, count)],
                    send.at[it, 1, s, y], recv.at[it, 1, inv_x[s], INV_Y[y]], device))
            for group in (0, 1):
                sz_ref[it, s, group] = both[128 * group:128 * group + 128, 128:256].T[0:16]
            for t, y, side, exists, device in side_near:
                if t != s:
                    continue
                rows = pl.ds(8 * side, 8)
                start(exists, remote(
                    sz_ref.at[it, s, min(y, 1), rows],
                    rz_ref.at[it, inv_x[s], INV_Y[y], rows],
                    z_send.at[it, 1, s, y, side], z_recv.at[it, 1, inv_x[s], INV_Y[y], 1 - side],
                    device))
        if it == 0:
            started.extend(view_sends)
        drain()
        for s, y, side, exists, device in side_near:
            rows = pl.ds(8 - 8 * side, 8)
            under(exists, lambda s=s, y=y, side=side, rows=rows, device=device: remote(
                sz_ref.at[it, s, 0, rows], rz_ref.at[it, s, y, rows],
                z_send.at[it, 1, s, y, side], z_recv.at[it, 1, s, y, side], device)().wait_recv())
        strips = jnp.zeros((16, 128), F32)
        for s in range(slots):
            strips = strips + rz_ref[it, s, 0]
            strips = strips + jnp.where(half, rz_ref[it, s, 2], rz_ref[it, s, 1])
        edge = jnp.concatenate([strips[0:8], jnp.zeros((112, 128), F32), strips[8:16]], axis=0)
        own_total = own_total + edge.T
        for s, y, exists, device in near:
            count = ROWS[y][1]
            under(exists, lambda s=s, y=y, count=count, device=device: remote(
                rc_ref.at[it, s, y, pl.ds(0, count)], rc_ref.at[it, s, y, pl.ds(0, count)],
                send.at[it, 1, s, y], recv.at[it, 1, s, y], device)().wait_recv())
        for s in range(slots):
            if s > 0:
                own_total = own_total + rc_ref[it, s, 0]
            own_total = own_total + jnp.concatenate(
                [rc_ref[it, s, 2, 0:64, :], rc_ref[it, s, 1, 0:64, :]], axis=0)
        estimate = estimate * (own_total / weight_sum)
        if it < ITERS - 1:
            u_ref[it + 1, 0, 0:128, :] = estimate
            send_estimate(it + 1, estimate)
    for y in range(16):
        out_ref[:, y, :] = estimate[8 * y:8 * y + 8, :]


def shards(sizes, views, estimate, psf, extents):
    n_gx, n_gy, n_gz = sizes
    V = views.shape[0]
    slots = 2 if n_gx == 2 else 3
    rows = slots * 256
    vmem = pl.BlockSpec(memory_space=pltpu.VMEM)
    whole = pl.BlockSpec(memory_space=pltpu.HBM)
    return pl.pallas_call(
        functools.partial(kernel, sizes),
        out_shape=jax.ShapeDtypeStruct(estimate.shape, F32),
        in_specs=[whole] * 4,
        out_specs=vmem,
        scratch_shapes=[
            pltpu.SMEM(psf.shape, F32),
            pltpu.SMEM((3, 2, V), jnp.int32),
            pltpu.VMEM(estimate.shape, F32),
            pltpu.VMEM((n_gz,) + views.shape[:3] + (128,), F32),
            pltpu.VMEM((V, 128, 128), F32),
            pltpu.VMEM((V * 128, 3 * rows), BF16),
            pltpu.VMEM((V, rows, 384), BF16),
            pltpu.VMEM((V, 768, 128), BF16),
            pltpu.VMEM((V, 384, 256), BF16),
            pltpu.VMEM((V, rows, 256), F32),
            pltpu.VMEM((ITERS, slots, 256, 128), F32),
            pltpu.VMEM((ITERS, slots, 3, 16, 128), F32),
            pltpu.VMEM((ITERS, 16, 128), F32),
            pltpu.VMEM((ITERS, slots, 256, 128), F32),
            pltpu.VMEM((ITERS, slots, 2, 16, 128), F32),
            pltpu.VMEM((ITERS, slots, 3, 128, 128), F32),
            pltpu.VMEM((ITERS, slots, 3, 16, 128), F32),
            pltpu.SemaphoreType.DMA((3,)),
            pltpu.SemaphoreType.DMA((n_gz,)),
            pltpu.SemaphoreType.DMA((n_gz,)),
            pltpu.SemaphoreType.DMA((ITERS, 2, slots, 3)),
            pltpu.SemaphoreType.DMA((ITERS, 2, slots, 3)),
            pltpu.SemaphoreType.DMA((ITERS, 2, slots, 3, 2)),
            pltpu.SemaphoreType.DMA((ITERS, 2, slots, 3, 2)),
        ],
        compiler_params=pltpu.CompilerParams(
            collective_id=0, has_side_effects=True, vmem_limit_bytes=60 * 1024 * 1024
        ),
    )(psf, extents.transpose(1, 2, 0), views, estimate)


def solution(mesh):
    sizes = (mesh.shape["gx"], mesh.shape["gy"], mesh.shape["gz"])
    placed = (P(None, "gx", ("gy", "gz"), None), P("gx", "gy", "gz"), P(), P())
    return jax.shard_map(
        functools.partial(shards, sizes), mesh=mesh, in_specs=placed,
        out_specs=P("gx", "gy", "gz"), check_vma=False,
    )
```

```python
import functools

import jax
import jax.numpy as jnp
from jax import lax
from jax.experimental import pallas as pl
from jax.experimental.pallas import tpu as pltpu
from jax.sharding import PartitionSpec as P

H = 8
K = 17
ITERS = 2
MESH = pl.DeviceIdType.MESH
F32 = jnp.float32
BF16 = jnp.bfloat16
NOWHERE = -100000
INV_Y = (0, 2, 1)
ROWS = ((0, 128), (128, 64), (192, 64))


def iota(shape, dim):
    return lax.broadcasted_iota(jnp.int32, shape, dim)


def split(value):
    high = value.astype(BF16)
    low = (value - high.astype(F32)).astype(BF16)
    return high, low


def wide(value):
    high, low = split(value)
    return jnp.concatenate([high, low, high], axis=1)


def tall(value):
    high, low = split(value)
    return jnp.concatenate([high, high, low], axis=0)


def z_place(index):
    return jnp.where(
        index < 128 + H,
        index,
        jnp.where(index < 128 + 2 * H, index - 128 - 2 * H, NOWHERE),
    )


def y_place(index):
    return jnp.where(index < 24, index, index - 32)


def pick(offset, tap):
    total = jnp.zeros(offset.shape, F32)
    for t in range(K):
        total = jnp.where(offset == t, tap(t), total)
    return total


def kernel(
    sizes, psf_in, extents_in, views_ref, est_ref, out_ref,
    psf_ref, extents_ref, est_in, images, image, forth, back, z_forth, z_back, weights, u_ref, z_ref, z_own, s_ref, sz_ref,
    rc_ref, rz_ref, est_sem, view_send, view_recv, send, recv, z_send, z_recv,
):
    n_gx, n_gy, n_gz = sizes
    V = image.shape[0]
    gx, gy, gz = lax.axis_index("gx"), lax.axis_index("gy"), lax.axis_index("gz")
    if n_gx == 2:
        x_targets = (gx, 1 - gx)
        x_exists = (None, None)
        x_offset = (0, H - 2 * H * gx)
        inv_x = (0, 1)
    else:
        x_targets = (gx, gx + 1, gx - 1)
        x_exists = (None, gx < n_gx - 1, gx > 0)
        x_offset = (0, H, -H)
        inv_x = (0, 2, 1)
    slots = len(x_targets)
    y_targets = (gy, gy + 1, gy - 1)
    y_exists = (None, gy < n_gy - 1, gy > 0)
    z_targets = (gz + 1, gz - 1)
    z_exists = (gz < n_gz - 1, gz > 0)
    near = []
    for s in range(slots):
        for y in range(3):
            if s == 0 and y == 0:
                continue
            exists = x_exists[s]
            if y_exists[y] is not None:
                exists = y_exists[y] if exists is None else exists & y_exists[y]
            near.append((s, y, exists, {"gx": x_targets[s], "gy": y_targets[y], "gz": gz}))
    side_near = []
    for s in range(slots):
        for y in range(3):
            for side in range(2):
                exists = z_exists[side]
                for other in (x_exists[s], y_exists[y]):
                    if other is not None:
                        exists = exists & other
                device = {"gx": x_targets[s], "gy": y_targets[y], "gz": z_targets[side]}
                side_near.append((s, y, side, exists, device))
    started = []

    def under(exists, do):
        if exists is None:
            do()
        else:
            pl.when(exists)(do)

    def start(exists, make):
        under(exists, lambda: make().start())
        started.append((exists, make))

    def drain():
        for exists, make in started:
            under(exists, lambda make=make: make().wait_send())
        started.clear()

    def remote(src, dst, s_sem, r_sem, device):
        return lambda: pltpu.make_async_remote_copy(
            src_ref=src, dst_ref=dst, send_sem=s_sem, recv_sem=r_sem,
            device_id=device, device_id_type=MESH,
        )

    est_copy = pltpu.make_async_copy(est_ref, est_in, est_sem.at[0])
    psf_copy = pltpu.make_async_copy(psf_in, psf_ref, est_sem.at[1])
    extents_copy = pltpu.make_async_copy(extents_in, extents_ref, est_sem.at[2])
    est_copy.start()
    barrier = pltpu.get_barrier_semaphore()
    expected = jnp.int32(n_gz - 1)
    for s, y, side, exists, device in side_near:
        if s == 0 and y == 0:
            continue
        under(exists, functools.partial(
            pl.semaphore_signal, barrier, inc=1, device_id=device, device_id_type=MESH))
        expected = expected + exists.astype(jnp.int32)
    for k in range(1, n_gz):
        pl.semaphore_signal(
            barrier, inc=1, device_id={"gx": gx, "gy": gy, "gz": lax.rem(gz + k, n_gz)},
            device_id_type=MESH,
        )
    for s, y, exists, device in near:
        under(exists, functools.partial(
            pl.semaphore_signal, barrier, inc=1, device_id=device, device_id_type=MESH))
        expected = expected + (1 if exists is None else exists.astype(jnp.int32))

    psf_copy.start()
    extents_copy.start()
    own_views = pltpu.make_async_copy(
        views_ref.at[:, :, :, pl.ds(pl.multiple_of(gz * 128, 128), 128)],
        images.at[gz], view_recv.at[0],
    )
    own_views.start()

    def zero_side(s, y, side):
        first = 8 * side
        for it in range(ITERS):
            z_ref[it, s, y, first:first + 8, :] = jnp.zeros((8, 128), F32)
            rz_ref[it, s, y, 8 - first:16 - first, :] = jnp.zeros((8, 128), F32)

    for s, y, side, exists, device in side_near:
        pl.when(jnp.logical_not(exists))(functools.partial(zero_side, s, y, side))

    def zero_near(s, y):
        first, count = ROWS[y]
        for it in range(ITERS):
            u_ref[it, s, first:first + count, :] = jnp.zeros((count, 128), F32)
            rc_ref[it, s, y, 0:count, :] = jnp.zeros((count, 128), F32)

    for s, y, exists, device in near:
        if exists is not None:
            pl.when(jnp.logical_not(exists))(functools.partial(zero_near, s, y))

    est_copy.wait()
    for y in range(16):
        u_ref[0, 0, 8 * y:8 * y + 8, :] = est_in[:, y, :]
    estimate = u_ref[0, 0, 0:128, :]

    def send_estimate(it, value):
        if it == 0:
            pl.semaphore_wait(barrier, expected)
        for s, y, exists, device in near[::-1]:
            source = (0, 64, 0)[y]
            first, count = ROWS[INV_Y[y]]
            start(exists, remote(
                u_ref.at[it, 0, pl.ds(source, count)],
                u_ref.at[it, inv_x[s], pl.ds(first, count)],
                send.at[it, 0, s, y], recv.at[it, 0, inv_x[s], INV_Y[y]], device))
        turned = value.T
        z_own[it, 0:8, :] = turned[0:8]
        z_own[it, 8:16, :] = turned[120:128]
        for s, y, side, exists, device in side_near[::-1]:
            rows = pl.ds(8 - 8 * side, 8)
            start(exists, remote(
                z_own.at[it, rows], z_ref.at[it, inv_x[s], INV_Y[y], rows],
                z_send.at[it, 0, s, y, side], z_recv.at[it, 0, inv_x[s], INV_Y[y], 1 - side],
                device))

    send_estimate(0, estimate)
    halo_sends = list(started)
    started.clear()
    for k in range(1, n_gz):
        target = lax.rem(gz + k, n_gz)
        start(None, remote(
            views_ref.at[:, :, :, pl.ds(pl.multiple_of(target * 128, 128), 128)],
            images.at[gz], view_send.at[k], view_recv.at[k],
            {"gx": gx, "gy": gy, "gz": target}))

    view_sends = list(started)
    started[:] = halo_sends

    def build(v, unused):
        def taps(axis):
            return lambda t: psf_ref[v, axis, t]

        scale = jnp.float32(1.0)
        for axis in range(3):
            total = psf_ref[v, axis, 0]
            for t in range(1, K):
                total = total + psf_ref[v, axis, t]
            scale = scale * total
        inverse = 1.0 / jnp.full((8, 128), scale, F32)
        z_band = pick(z_place(iota((144, 128), 0)) - iota((144, 128), 1) + H, taps(2))
        z_band = z_band * inverse[0:1]
        z_band = jnp.concatenate([z_band, jnp.zeros((112, 128), F32)], axis=0)
        z_forth[v] = tall(z_band)
        z_band_t = jnp.concatenate([z_band[0:128].T, z_band[128:256].T], axis=1)
        z_back[v] = tall(z_band_t)
        own = pl.ds(pl.multiple_of(v * 128, 128), 128)
        lane = iota((16, 256), 1)
        y_rows = pick(y_place(lane // 8) - iota((16, 256), 0) + H, taps(1))
        y_rows_t = pick(y_place(iota((32, 128), 0)) - iota((32, 128), 1) // 8 + H, taps(1))
        row = iota((8, 128), 0)
        column = iota((8, 128), 1) % 8
        for s in range(slots):
            x_tile = pick(x_offset[s] + column - row + H, taps(0))
            x_tile_t = pick(x_offset[s] + row - column + H, taps(0))
            for group in range(2):
                block = y_rows[:, None, 128 * group:128 * group + 128] * x_tile[None]
                high, low = split(block.reshape(128, 128))
                first = s * 256 + group * 128
                width = slots * 256
                forth[own, first:first + 128] = high
                forth[own, width + first:width + first + 128] = low
                forth[own, 2 * width + first:2 * width + first + 128] = high
                block = y_rows_t[16 * group:16 * group + 16, None, :] * x_tile_t[None]
                high, low = split(block.reshape(128, 128))
                back[v, first:first + 128, 0:128] = high
                back[v, first:first + 128, 128:256] = low
                back[v, first:first + 128, 256:384] = high
        z_abs = gz * 128 + z_place(iota((8, 256), 1))
        in_z = (z_abs >= extents_ref[2, 0, v]) & (z_abs < extents_ref[2, 1, v])
        z_part = jnp.where(in_z, F32(0.75), F32(0.0))[0:1]
        for s in range(slots):
            rows = iota((256, 128), 0)
            y_abs = gy * 16 + y_place(rows // 8)
            x_abs = gx * 8 + x_offset[s] + rows % 8
            inside = (y_abs >= extents_ref[1, 0, v]) & (y_abs < extents_ref[1, 1, v])
            inside = inside & (x_abs >= extents_ref[0, 0, v]) & (x_abs < extents_ref[0, 1, v])
            flag = jnp.where(inside, F32(1.0), F32(0.0))
            weights[v, s * 256:s * 256 + 256, 0:128] = flag * z_part[:, 0:128] + 0.25
            weights[v, s * 256:s * 256 + 256, 128:256] = flag * z_part[:, 128:256] + 0.25
        return unused

    psf_copy.wait()
    extents_copy.wait()

    def build_three(i, unused):
        for k in range(3):
            unused = build(3 * i + k, unused)
        return unused

    lax.fori_loop(0, V // 3, build_three, 0)
    for v in range(V - V % 3, V):
        build(v, 0)
    weight_sum = weights[0, 0:128, 0:128]
    for v in range(1, V):
        weight_sum = weight_sum + weights[v, 0:128, 0:128]

    half = iota((16, 128), 1) < 64
    for it in range(ITERS):
        drain()
        for s, y, exists, device in near:
            first, count = ROWS[y]
            under(exists, lambda s=s, y=y, first=first, count=count, device=device: remote(
                u_ref.at[it, s, pl.ds(first, count)], u_ref.at[it, s, pl.ds(first, count)],
                send.at[it, 0, s, y], recv.at[it, 0, s, y], device)().wait_recv())
        for s, y, side, exists, device in side_near:
            rows = pl.ds(8 * side, 8)
            under(exists, lambda s=s, y=y, side=side, rows=rows, device=device: remote(
                z_own.at[it, rows], z_ref.at[it, s, y, rows],
                z_send.at[it, 0, s, y, side], z_recv.at[it, 0, s, y, side], device)().wait_recv())
        pieces = []
        fill = jnp.zeros((112, 128), F32)
        for s in range(slots):
            halo = jnp.where(half, z_ref[it, s, 1], z_ref[it, s, 2])
            for group, strip in enumerate((z_ref[it, s, 0], halo)):
                turned = jnp.concatenate([strip, fill], axis=0).T
                middle = u_ref[it, s, 128 * group:128 * group + 128, :]
                pieces.append(jnp.concatenate([middle, turned], axis=1))
        padded = tall(jnp.concatenate(pieces, axis=0))
        blurred = []
        across = jnp.dot(forth[...], padded, preferred_element_type=F32)
        for v in range(V):
            lines = wide(across[128 * v:128 * v + 128])
            blurred.append(jnp.dot(lines, z_forth[v], preferred_element_type=F32))
        if it == 0:
            own_views.wait()
            for k in range(1, n_gz):
                remote(
                    images.at[0], images.at[lax.rem(gz + n_gz - k, n_gz)],
                    view_send.at[k], view_recv.at[k],
                    {"gx": gx, "gy": gy, "gz": lax.rem(gz + n_gz - k, n_gz)})().wait_recv()
            per = 16 // n_gz
            for v in range(V):
                for g in range(n_gz):
                    for yy in range(per):
                        first = 8 * (per * g + yy)
                        image[v, first:first + 8, :] = images[g, v, :, yy, :]
        spread = []
        for v in range(V):
            ratio = image[v] / blurred[v]
            lines = jnp.dot(wide(ratio), z_back[v], preferred_element_type=F32)
            spread.append(tall(lines))

        def summed(first):
            total = None
            for v in range(V):
                part = jnp.dot(
                    back[v, first:first + 256, :], spread[v], preferred_element_type=F32)
                part = part * weights[v, first:first + 256, :]
                total = part if total is None else total + part
            return total

        for s in range(slots - 1, -1, -1):
            both = summed(s * 256)
            if s == 0:
                own_total = both[0:128, 0:128]
                s_ref[it, s, 128:256, :] = both[128:256, 0:128]
            else:
                s_ref[it, s] = both[:, 0:128]
            for t, y, exists, device in near:
                if t != s:
                    continue
                first, count = ROWS[y]
                start(exists, remote(
                    s_ref.at[it, s, pl.ds(first, count)],
                    rc_ref.at[it, inv_x[s], INV_Y[y], pl.ds(0, count)],
                    send.at[it, 1, s, y], recv.at[it, 1, inv_x[s], INV_Y[y]], device))
            for group in (0, 1):
                sz_ref[it, s, group] = both[128 * group:128 * group + 128, 128:256].T[0:16]
            for t, y, side, exists, device in side_near:
                if t != s:
                    continue
                rows = pl.ds(8 * side, 8)
                start(exists, remote(
                    sz_ref.at[it, s, min(y, 1), rows],
                    rz_ref.at[it, inv_x[s], INV_Y[y], rows],
                    z_send.at[it, 1, s, y, side], z_recv.at[it, 1, inv_x[s], INV_Y[y], 1 - side],
                    device))
        if it == 0:
            started.extend(view_sends)
        drain()
        for s, y, side, exists, device in side_near:
            rows = pl.ds(8 - 8 * side, 8)
            under(exists, lambda s=s, y=y, side=side, rows=rows, device=device: remote(
                sz_ref.at[it, s, 0, rows], rz_ref.at[it, s, y, rows],
                z_send.at[it, 1, s, y, side], z_recv.at[it, 1, s, y, side], device)().wait_recv())
        strips = jnp.zeros((16, 128), F32)
        for s in range(slots):
            strips = strips + rz_ref[it, s, 0]
            strips = strips + jnp.where(half, rz_ref[it, s, 2], rz_ref[it, s, 1])
        edge = jnp.concatenate([strips[0:8], jnp.zeros((112, 128), F32), strips[8:16]], axis=0)
        own_total = own_total + edge.T
        for s, y, exists, device in near:
            count = ROWS[y][1]
            under(exists, lambda s=s, y=y, count=count, device=device: remote(
                rc_ref.at[it, s, y, pl.ds(0, count)], rc_ref.at[it, s, y, pl.ds(0, count)],
                send.at[it, 1, s, y], recv.at[it, 1, s, y], device)().wait_recv())
        for s in range(slots):
            if s > 0:
                own_total = own_total + rc_ref[it, s, 0]
            own_total = own_total + jnp.concatenate(
                [rc_ref[it, s, 2, 0:64, :], rc_ref[it, s, 1, 0:64, :]], axis=0)
        estimate = estimate * (own_total / weight_sum)
        if it < ITERS - 1:
            u_ref[it + 1, 0, 0:128, :] = estimate
            send_estimate(it + 1, estimate)
    for y in range(16):
        out_ref[:, y, :] = estimate[8 * y:8 * y + 8, :]


def shards(sizes, views, estimate, psf, extents):
    n_gx, n_gy, n_gz = sizes
    V = views.shape[0]
    slots = 2 if n_gx == 2 else 3
    rows = slots * 256
    vmem = pl.BlockSpec(memory_space=pltpu.VMEM)
    whole = pl.BlockSpec(memory_space=pltpu.HBM)
    return pl.pallas_call(
        functools.partial(kernel, sizes),
        out_shape=jax.ShapeDtypeStruct(estimate.shape, F32),
        in_specs=[whole] * 4,
        out_specs=vmem,
        scratch_shapes=[
            pltpu.SMEM(psf.shape, F32),
            pltpu.SMEM((3, 2, V), jnp.int32),
            pltpu.VMEM(estimate.shape, F32),
            pltpu.VMEM((n_gz,) + views.shape[:3] + (128,), F32),
            pltpu.VMEM((V, 128, 128), F32),
            pltpu.VMEM((V * 128, 3 * rows), BF16),
            pltpu.VMEM((V, rows, 384), BF16),
            pltpu.VMEM((V, 768, 128), BF16),
            pltpu.VMEM((V, 384, 256), BF16),
            pltpu.VMEM((V, rows, 256), F32),
            pltpu.VMEM((ITERS, slots, 256, 128), F32),
            pltpu.VMEM((ITERS, slots, 3, 16, 128), F32),
            pltpu.VMEM((ITERS, 16, 128), F32),
            pltpu.VMEM((ITERS, slots, 256, 128), F32),
            pltpu.VMEM((ITERS, slots, 2, 16, 128), F32),
            pltpu.VMEM((ITERS, slots, 3, 128, 128), F32),
            pltpu.VMEM((ITERS, slots, 3, 16, 128), F32),
            pltpu.SemaphoreType.DMA((3,)),
            pltpu.SemaphoreType.DMA((n_gz,)),
            pltpu.SemaphoreType.DMA((n_gz,)),
            pltpu.SemaphoreType.DMA((ITERS, 2, slots, 3)),
            pltpu.SemaphoreType.DMA((ITERS, 2, slots, 3)),
            pltpu.SemaphoreType.DMA((ITERS, 2, slots, 3, 2)),
            pltpu.SemaphoreType.DMA((ITERS, 2, slots, 3, 2)),
        ],
        compiler_params=pltpu.CompilerParams(
            collective_id=0, has_side_effects=True, vmem_limit_bytes=60 * 1024 * 1024
        ),
    )(psf, extents.transpose(1, 2, 0), views, estimate)


def solution(mesh):
    sizes = (mesh.shape["gx"], mesh.shape["gy"], mesh.shape["gz"])
    placed = (P(None, "gx", ("gy", "gz"), None), P("gx", "gy", "gz"), P(), P())
    return jax.shard_map(
        functools.partial(shards, sizes), mesh=mesh, in_specs=placed,
        out_specs=P("gx", "gy", "gz"), check_vma=False,
    )
```
